32 devices in a mesh: gx: 8 (over y, x, core), gy: 4 (over z).
Axes of the slice: x: 2, y: 2, z: 4, core: 2. Of those that a mesh axis runs over, the one named last changes fastest.
Arguments:
- wave_state: float32 [3, 128, 512, 128], P(None, 'gy', 'gx'), may hold values from -6 to 6
- tracers: float32 [6, 128, 512, 128], P(None, 'gy', 'gx'), may hold values from -6 to 6
- eddy: float32 [128, 512, 128], P('gy', 'gx'), may hold values from 0.05 to 2
- cost_class: int32 [128, 512], P('gy', 'gx'), may hold values from 0 to 3
- span_slot: int32 [128, 512], P('gy', 'gx'), may hold values from 0 to 4095, as said below
Outputs:
- wave_after: float32 [3, 128, 512, 128], P(None, 'gy', 'gx')
- tracers_after: float32 [6, 128, 512, 128], P(None, 'gy', 'gx')
- span_tendency: float32 [32, 32, 128, 128], P(('gx', 'gy'))
The draws below stay inside these ranges and needn't reach their ends.
Inputs may be any that keep to these rules, and one draw needn't show every extreme that they name: span_slot is owner * 128 + slot, with owner an index along gx+gy and slot below 128; among the columns of one device no two hold the same value; every owner receives all 128 slots from at least one device.
All inputs are finite; a program needn't handle non-finite values.
Results may differ from the reference program's by a relative error of at most 0.00002.
Values sent between devices are 32-bit elements; how exact they have to be, the bound alone decides.
A program may use at most 192 MiB of HBM per device.

```python
import math
import jax
import jax.numpy as jnp
from jax import lax

LAT_DEV = 32
LON_DEV = 64
LEVELS = 128
TRACERS = 6
SUBSTEPS = 4
NLAT = 128
NLON = 512
CAP = 128
N_GX = 8
N_GY = 4
DEVICES = 32


def strong_columns(key):
    picks = jax.random.randint(jax.random.fold_in(key, 7), (NLAT, NLON), 0, 16)
    return picks == 0


def draw_eddy(key, part):
    strong = strong_columns(key)
    key = jax.random.fold_in(key, 21)
    shape = (NLAT, NLON, LEVELS)
    weak = jnp.exp(jax.random.uniform(jax.random.fold_in(key, 1), shape, jnp.float32, math.log(0.05), math.log(2.0)))
    heavy = jnp.exp(jax.random.uniform(jax.random.fold_in(key, 2), shape, jnp.float32, math.log(1.5), math.log(2.0)))
    values = jnp.where(strong[:, :, None], heavy, weak)
    return jnp.clip(values, 0.05, 2.0).astype(jnp.float32)


def draw_cost_class(key, part):
    strong = strong_columns(key)
    key = jax.random.fold_in(key, 22)
    base = jax.random.randint(key, (NLAT, NLON), 0, 4)
    return jnp.where(strong, 3, base).astype(jnp.int32)


def draw_span_slot(key, part):
    key = jax.random.fold_in(key, 11)
    pool = DEVICES * CAP
    columns = LAT_DEV * LON_DEV
    offset = jax.random.randint(jax.random.fold_in(key, 1), (), 0, DEVICES)
    favored = jax.random.permutation(jax.random.fold_in(key, 2), DEVICES) < DEVICES // 4
    entries = jnp.arange(pool, dtype=jnp.int32)
    owners = entries // CAP

    def one_device(index):
        subkey = jax.random.fold_in(key, 100 + index)
        forced = (index + offset) % DEVICES
        score = jax.random.permutation(jax.random.fold_in(subkey, 1), pool).astype(jnp.int32)
        score = score - jnp.where(favored[owners], pool // 2, 0) - jnp.where(owners == forced, 2 * pool, 0)
        ordering = jnp.argsort(score, stable=True)
        chosen = ordering[:columns].astype(jnp.int32)
        return jax.random.permutation(jax.random.fold_in(subkey, 2), chosen)
    table = jax.vmap(one_device)(jnp.arange(DEVICES, dtype=jnp.int32))
    table = table.reshape(N_GX, N_GY, LAT_DEV, LON_DEV).transpose(1, 2, 0, 3)
    return table.reshape(N_GY * LAT_DEV, N_GX * LON_DEV).astype(jnp.int32)


def block_levels(own_key, shape, split, low, largest):
    def one(position, shards_of):
        heights = jax.random.uniform(jax.random.fold_in(jax.random.fold_in(own_key, 6), position), (shards_of,), jnp.float32, low / len(split), largest / len(split))
        return jnp.repeat(jnp.exp(heights), shape[position] // shards_of).reshape((-1,) + (1,) * (len(shape) - position - 1))

    factor_of = one(*split[0])
    for cut in split[1:]:
        factor_of = factor_of * one(*cut)
    return factor_of


def centred(stream_key, shape, width, bound, cuts=(), kind=jnp.bfloat16):
    loudness = block_levels(stream_key, shape, cuts, -0.22, 0.18) if cuts else 1.0
    result = jax.random.normal(stream_key, shape, jnp.float32) * width * loudness
    return jnp.minimum(jnp.maximum(result, -bound), bound).astype(kind)


def setup_inputs(seed: int = 0) -> dict:
    keys = jax.random.split(jax.random.key(seed), 6)
    wave_state = centred(keys[0], (3, NLAT, NLON, LEVELS), 1.0, 6.0, ((1, 4), (2, 8)), jnp.float32)
    tracers = centred(keys[1], (TRACERS, NLAT, NLON, LEVELS), 1.0, 6.0, ((1, 4), (2, 8)), jnp.float32)
    eddy = draw_eddy(jax.random.fold_in(keys[5], 71), 0)
    cost_class = draw_cost_class(jax.random.fold_in(keys[5], 71), 0)
    span_slot = draw_span_slot(jax.random.fold_in(keys[5], 71), 0)
    return dict(wave_state=wave_state, tracers=tracers, eddy=eddy, cost_class=cost_class, span_slot=span_slot)


COURANT = 0.6


def wave_step(padded):
    press = padded[0]
    east = padded[1]
    north = padded[2]
    east_new = east[:, :-1] - COURANT * (press[:, 1:] - press[:, :-1])
    north_new = north[:-1, :] - COURANT * (press[1:, :] - press[:-1, :])
    press_new = press[1:-1, 1:-1] - COURANT * ((east_new[1:-1, 1:] - east_new[1:-1, :-1]) + (north_new[1:, 1:-1] - north_new[:-1, 1:-1]))
    return jnp.stack([press_new, east_new[1:-1, 1:], north_new[1:, 1:-1]])


def shear_factor(wave):
    east = wave[1]
    north = wave[2]
    shear = jnp.abs(east[:, :, 1:] - east[:, :, :-1]) + jnp.abs(north[:, :, 1:] - north[:, :, :-1])
    shear = jnp.concatenate([shear, jnp.zeros_like(shear[:, :, :1])], axis=2)
    return 1.0 + shear


def implicit_mix(mixing_rows, tracer_rows):
    mixing = mixing_rows.T
    zero_row = jnp.zeros_like(mixing[:1])
    below = jnp.concatenate([zero_row, mixing[:-1]], 0)
    above = jnp.concatenate([mixing[:-1], zero_row], 0)
    diagonal = 1.0 + below + above
    rhs_levels = jnp.transpose(tracer_rows, (2, 0, 1))

    def forward(carry, level):
        c_prev, d_prev = carry
        lower, upper, middle, right = level
        denom = middle + lower * c_prev
        c_now = -upper / denom
        d_now = (right + lower[None] * d_prev) / denom[None]
        return (c_now, d_now), (c_now, d_now)

    start = (jnp.zeros_like(mixing[0]), jnp.zeros_like(rhs_levels[0]))
    unused, (c_all, d_all) = lax.scan(forward, start, (below, above, diagonal, rhs_levels))

    def backward(x_next, level):
        c_now, d_now = level
        x_now = d_now - c_now[None] * x_next
        return x_now, x_now

    unused, solved = lax.scan(backward, jnp.zeros_like(rhs_levels[0]), (c_all, d_all), reverse=True)
    return jnp.transpose(solved, (1, 2, 0))


def reference(wave_state, tracers, eddy, cost_class, span_slot):
    wave = wave_state
    for step in range(SUBSTEPS):
        padded = jnp.concatenate([wave[:, :, -1:], wave, wave[:, :, :1]], axis=2)
        padded = jnp.pad(padded, ((0, 0), (1, 1), (0, 0), (0, 0)))
        wave = wave_step(padded)
    mixing = eddy * (1.0 + cost_class.astype(eddy.dtype))[:, :, None] * shear_factor(wave)
    mix_blocks = mixing.reshape(N_GY, LAT_DEV * NLON, LEVELS)
    tracer_blocks = tracers.reshape(TRACERS, N_GY, LAT_DEV * NLON, LEVELS).transpose(1, 0, 2, 3)
    solved = lax.map(lambda pair: implicit_mix(pair[0], pair[1]), (mix_blocks, tracer_blocks))
    tracers_after = solved.transpose(1, 0, 2, 3).reshape(TRACERS, NLAT, NLON, LEVELS)
    change = jnp.sum(tracers_after - tracers, axis=0)
    lat_index = jnp.arange(NLAT, dtype=jnp.int32)[:, None]
    lon_index = jnp.arange(NLON, dtype=jnp.int32)[None, :]
    source = (lon_index // LON_DEV) * N_GY + lat_index // LAT_DEV
    owner = span_slot // CAP
    slot = span_slot % CAP
    target = (owner * (DEVICES * CAP) + source * CAP + slot).reshape(-1)
    span = jnp.zeros((DEVICES * DEVICES * CAP, LEVELS), tracers.dtype)
    span = span.at[target].set(change.reshape(-1, LEVELS))
    return wave, tracers_after, span.reshape(DEVICES, DEVICES, CAP, LEVELS)
```

```python
import functools

import jax
import jax.numpy as jnp
from jax import lax
from jax.experimental import pallas as pl
from jax.experimental.pallas import tpu as pltpu
from jax.sharding import PartitionSpec as P

SUBSTEPS = 4
COURANT = 0.6
HALO = 4
LANE = 128
MESH = pl.DeviceIdType.MESH
ANY = pl.BlockSpec(memory_space=pl.ANY)
VMEM = pl.BlockSpec(memory_space=pltpu.VMEM)
SMEM = pl.BlockSpec(memory_space=pltpu.SMEM)


def exchange_kernel(
    ngx, ngy, wave_ref, tracers_ref, padded_ref, total_ref, loaded, send_sem, recv_sem, load_sem
):
    gx = lax.axis_index("gx")
    gy = lax.axis_index("gy")
    rows, cols = wave_ref.shape[1:3]
    tracer_count = tracers_ref.shape[0]
    groups = total_ref.shape[0] // LANE
    east = lax.rem(gx + 1, ngx)
    west = lax.rem(gx + ngx - 1, ngx)
    loads = [
        pltpu.make_async_copy(tracers_ref.at[t], loaded.at[t], load_sem.at[t])
        for t in range(tracer_count)
    ]
    for load in loads:
        load.start()
    own = pltpu.make_async_copy(
        wave_ref,
        padded_ref.at[:, pl.ds(HALO, rows), pl.ds(8, cols), :],
        load_sem.at[tracer_count],
    )
    own.start()

    barrier = pltpu.get_barrier_semaphore()
    for there in (west, east):
        pl.semaphore_signal(barrier, inc=1, device_id=(there, gy), device_id_type=MESH)

    @pl.when(gy > 0)
    def _():
        for there in (west, gx, east):
            pl.semaphore_signal(barrier, inc=1, device_id=(there, gy - 1), device_id_type=MESH)

    @pl.when(gy < ngy - 1)
    def _():
        for there in (west, gx, east):
            pl.semaphore_signal(barrier, inc=1, device_id=(there, gy + 1), device_id_type=MESH)

    peers = 2 + jnp.where(gy > 0, 3, 0) + jnp.where(gy < ngy - 1, 3, 0)
    pl.semaphore_wait(barrier, peers)

    lon_parts = {
        -1: (pl.ds(0, 8), pl.ds(cols + 8, 8)),
        0: (pl.ds(0, cols), pl.ds(8, cols)),
        1: (pl.ds(cols - 8, 8), pl.ds(0, 8)),
    }
    lat_parts = {
        -1: (pl.ds(0, HALO), pl.ds(rows + HALO, HALO)),
        0: (pl.ds(0, rows), pl.ds(HALO, rows)),
        1: (pl.ds(rows - HALO, HALO), pl.ds(0, HALO)),
    }
    lon_device = {-1: west, 0: gx, 1: east}

    def copy_to(dy, dx):
        index = (dy + 1) * 3 + dx + 1
        lat_from, lat_to = lat_parts[dy]
        lon_from, lon_to = lon_parts[dx]
        return pltpu.make_async_remote_copy(
            src_ref=wave_ref.at[:, lat_from, lon_from, :],
            dst_ref=padded_ref.at[:, lat_to, lon_to, :],
            send_sem=send_sem.at[index],
            recv_sem=recv_sem.at[index],
            device_id=(lon_device[dx], gy + dy),
            device_id_type=MESH,
        )

    @pl.when(gy > 0)
    def _():
        for dx in (0, -1, 1):
            copy_to(-1, dx).start()

    @pl.when(gy < ngy - 1)
    def _():
        for dx in (0, -1, 1):
            copy_to(1, dx).start()

    for dx in (-1, 1):
        copy_to(0, dx).start()

    for load in loads:
        load.wait()

    def transpose_group(b, carry):
        part = pl.ds(pl.multiple_of(b * LANE, LANE), LANE)
        value = loaded[0, part, :]
        for t in range(1, tracer_count):
            value = value + loaded[t, part, :]
        total_ref[pl.ds(b, LANE, stride=groups), :] = value.T
        return carry

    lax.fori_loop(0, groups, transpose_group, 0)
    own.wait()
    for dx in (-1, 1):
        copy_to(0, dx).wait()

    @pl.when(gy > 0)
    def _():
        for dx in (0, -1, 1):
            copy_to(-1, dx).wait_send()
            copy_to(1, dx).wait_recv()

    @pl.when(gy < ngy - 1)
    def _():
        for dx in (0, -1, 1):
            copy_to(1, dx).wait_send()
            copy_to(-1, dx).wait_recv()


def column_kernel(
    ngy,
    padded_ref,
    eddy_ref,
    class_ref,
    slot_ref,
    total_ref,
    wave_ref,
    mix_ref,
    inverse_ref,
    outgoing_ref,
    field,
    change,
    solved,
    sem,
):
    gy = lax.axis_index("gy")
    rows, cols, levels = eddy_ref.shape
    groups = rows * cols // LANE
    per_group = LANE // cols
    wide = cols + 16
    load = pltpu.make_async_copy(padded_ref, field.at[:, :, pl.ds(8, wide), :], sem)
    load.start()
    outgoing_ref[...] = jnp.zeros_like(outgoing_ref)
    load.wait()

    @pl.when(gy == 0)
    def _():
        field[:, pl.ds(0, HALO)] = jnp.zeros((3, HALO, wide + 16, levels), jnp.float32)

    @pl.when(gy == ngy - 1)
    def _():
        field[:, pl.ds(rows + HALO, HALO)] = jnp.zeros((3, HALO, wide + 16, levels), jnp.float32)

    here = pl.ds(8, wide)
    for step in range(SUBSTEPS):
        low = jnp.where(gy == 0, HALO, step + 1)
        high = jnp.where(gy == ngy - 1, rows + HALO, rows + 2 * HALO - 1 - step)
        north_before = field[2, low - 1, here] - COURANT * (
            field[0, low, here] - field[0, low - 1, here]
        )

        def one_row(i, north_below):
            press = field[0, i, here]
            east = field[1, i, here] - COURANT * (field[0, i, pl.ds(9, wide)] - press)
            north = field[2, i, here] - COURANT * (field[0, i + 1, here] - press)
            field[1, i, here] = east
            field[2, i, here] = north
            east_below = field[1, i, pl.ds(7, wide)]
            field[0, i, here] = press - COURANT * ((east - east_below) + (north - north_below))
            return north

        lax.fori_loop(low, high, one_row, north_before)

    lane = lax.broadcasted_iota(jnp.int32, (cols, levels), 1)
    own = pl.ds(16, cols)

    def one_group(b, carry):
        parts = []
        for r in range(per_group):
            i = b * per_group + r
            east = field[1, i + HALO, own]
            north = field[2, i + HALO, own]
            wave_ref[0, i] = field[0, i + HALO, own]
            wave_ref[1, i] = east
            wave_ref[2, i] = north
            shear = jnp.abs(pltpu.roll(east, levels - 1, 1) - east) + jnp.abs(
                pltpu.roll(north, levels - 1, 1) - north
            )
            parts.append(eddy_ref[i] * (1.0 + jnp.where(lane < levels - 1, shear, 0.0)))
        mix_ref[pl.ds(b, levels, stride=groups), :] = jnp.concatenate(parts, 0).T
        return carry

    lax.fori_loop(0, groups, one_group, 0)

    scale = 1.0 + class_ref[...].astype(jnp.float32)

    def level_rows(k):
        return pl.ds(pl.multiple_of(k * groups, groups), groups)

    def forward(k, carry):
        ratio_s, mix_below, value_below = carry
        at = level_rows(k)
        mix = jnp.where(k < levels - 1, mix_ref[at, :] * scale, 0.0)
        diagonal = 1.0 + ratio_s
        inverse = 1.0 / (diagonal + mix)
        value = (total_ref[at, :] + mix_below * value_below) * inverse
        mix_ref[at, :] = mix
        inverse_ref[at, :] = inverse
        solved[at, :] = value
        return mix * diagonal * inverse, mix, value

    zero = jnp.zeros((groups, LANE), jnp.float32)
    lax.fori_loop(0, levels, forward, (zero, zero, zero), unroll=4)

    def backward(n, above):
        at = level_rows(levels - 1 - n)
        value = solved[at, :] + mix_ref[at, :] * inverse_ref[at, :] * above
        solved[at, :] = value - total_ref[at, :]
        return value

    lax.fori_loop(0, levels, backward, zero, unroll=8)

    def back_group(b, carry):
        part = pl.ds(pl.multiple_of(b * LANE, LANE), LANE)
        change[part, :] = solved[pl.ds(b, levels, stride=groups), :].T
        return carry

    lax.fori_loop(0, groups, back_group, 0)

    def place(i, carry):
        for j in range(cols):
            outgoing_ref[pl.ds(slot_ref[i, j], 1), :] = change[pl.ds(i * cols + j, 1), :]
        return carry

    lax.fori_loop(0, rows, place, 0)


def tracer_kernel(
    ngx,
    ngy,
    tracers_ref,
    mix_hbm,
    inverse_hbm,
    outgoing_ref,
    after_ref,
    span_ref,
    loaded,
    stored,
    work,
    mix_ref,
    inverse_ref,
    send_sem,
    recv_sem,
    load_sem,
    store_sem,
    own_sem,
):
    devices = ngx * ngy
    gx = lax.axis_index("gx")
    gy = lax.axis_index("gy")
    me = gx * ngy + gy
    tracer_count, columns, levels = tracers_ref.shape
    groups = columns // LANE
    loads = [pltpu.make_async_copy(mix_hbm, mix_ref, own_sem.at[0])]
    loads.append(pltpu.make_async_copy(inverse_hbm, inverse_ref, own_sem.at[1]))
    own = pltpu.make_async_copy(outgoing_ref.at[me], span_ref.at[me], own_sem.at[2])

    def tracer_in(t):
        return pltpu.make_async_copy(tracers_ref.at[t], loaded.at[t], load_sem.at[t])

    def tracer_out(t):
        return pltpu.make_async_copy(stored.at[t], after_ref.at[t], store_sem.at[t])

    def partner(n):
        px = lax.rem(gx + n // ngy, ngx)
        py = lax.rem(gy + lax.rem(n, ngy), ngy)
        return px, py

    barrier = pltpu.get_barrier_semaphore()

    def greet(n, carry):
        pl.semaphore_signal(barrier, inc=1, device_id=partner(n), device_id_type=MESH)
        return carry

    lax.fori_loop(1, devices, greet, 0)
    for load in loads:
        load.start()
    own.start()
    for t in range(tracer_count):
        tracer_in(t).start()
    pl.semaphore_wait(barrier, devices - 1)

    def send(n):
        px, py = partner(n)
        return pltpu.make_async_remote_copy(
            src_ref=outgoing_ref.at[px * ngy + py],
            dst_ref=span_ref.at[me],
            send_sem=send_sem.at[n],
            recv_sem=recv_sem.at[n],
            device_id=(px, py),
            device_id_type=MESH,
        )

    def start_send(n, carry):
        send(n).start()
        return carry

    lax.fori_loop(1, devices, start_send, 0)
    for load in loads:
        load.wait()
    zero = jnp.zeros((groups, LANE), jnp.float32)

    def level_rows(k):
        return pl.ds(pl.multiple_of(k * groups, groups), groups)

    def one_tracer(t, carry):
        tracer_in(t).wait()

        def turn(b, carry):
            part = pl.ds(pl.multiple_of(b * LANE, LANE), LANE)
            work[pl.ds(b, levels, stride=groups), :] = loaded[t, part, :].T
            return carry

        lax.fori_loop(0, groups, turn, 0)

        def forward(k, carry):
            mix_below, value_below = carry
            at = level_rows(k)
            value = (work[at, :] + mix_below * value_below) * inverse_ref[at, :]
            work[at, :] = value
            return mix_ref[at, :], value

        lax.fori_loop(0, levels, forward, (zero, zero), unroll=8)

        def backward(n, above):
            at = level_rows(levels - 1 - n)
            value = work[at, :] + mix_ref[at, :] * inverse_ref[at, :] * above
            work[at, :] = value
            return value

        lax.fori_loop(0, levels, backward, zero, unroll=8)

        def turn_back(b, carry):
            part = pl.ds(pl.multiple_of(b * LANE, LANE), LANE)
            stored[t, part, :] = work[pl.ds(b, levels, stride=groups), :].T
            return carry

        lax.fori_loop(0, groups, turn_back, 0)
        tracer_out(t).start()
        return carry

    lax.fori_loop(0, tracer_count, one_tracer, 0)

    for t in range(tracer_count):
        tracer_out(t).wait()
    own.wait()

    def finish(n, carry):
        send(n).wait()
        return carry

    lax.fori_loop(1, devices, finish, 0)


def per_device(ngx, ngy, wave_state, tracers, eddy, cost_class, span_slot):
    rows, cols, levels = eddy.shape
    columns = rows * cols
    groups = columns // LANE
    devices = ngx * ngy
    capacity = max(2, (2 * columns + devices - 1) // devices)
    tracer_count = tracers.shape[0]
    f32 = jnp.float32
    flat = tracers.reshape(tracer_count, columns, levels)
    turned = jax.ShapeDtypeStruct((levels * groups, LANE), f32)
    dma = pltpu.SemaphoreType.DMA
    limit = 48 * 2**20

    padded, total = pl.pallas_call(
        functools.partial(exchange_kernel, ngx, ngy),
        out_shape=(
            jax.ShapeDtypeStruct((3, rows + 2 * HALO, cols + 16, levels), f32),
            turned,
        ),
        in_specs=[ANY, ANY],
        out_specs=(ANY, VMEM),
        scratch_shapes=[
            pltpu.VMEM((tracer_count, columns, levels), f32),
            dma((9,)),
            dma((9,)),
            dma((tracer_count + 1,)),
        ],
        compiler_params=pltpu.CompilerParams(
            collective_id=0, has_side_effects=True, vmem_limit_bytes=limit
        ),
        name="exchange",
    )(wave_state, flat)

    wave_after, mix, inverse, outgoing = pl.pallas_call(
        functools.partial(column_kernel, ngy),
        out_shape=(
            jax.ShapeDtypeStruct(wave_state.shape, f32),
            turned,
            turned,
            jax.ShapeDtypeStruct((devices * capacity, levels), f32),
        ),
        in_specs=[ANY, VMEM, VMEM, SMEM, VMEM],
        out_specs=(VMEM, VMEM, VMEM, VMEM),
        scratch_shapes=[
            pltpu.VMEM((3, rows + 2 * HALO, cols + 32, levels), f32),
            pltpu.VMEM((columns, levels), f32),
            pltpu.VMEM((levels * groups, LANE), f32),
            dma(()),
        ],
        compiler_params=pltpu.CompilerParams(vmem_limit_bytes=limit),
        name="columns",
    )(padded, eddy, cost_class.reshape(groups, LANE), span_slot, total)

    after, span = pl.pallas_call(
        functools.partial(tracer_kernel, ngx, ngy),
        out_shape=(
            jax.ShapeDtypeStruct((tracer_count, columns, levels), f32),
            jax.ShapeDtypeStruct((devices, capacity, levels), f32),
        ),
        in_specs=[ANY, ANY, ANY, ANY],
        out_specs=(ANY, ANY),
        scratch_shapes=[
            pltpu.VMEM((tracer_count, columns, levels), f32),
            pltpu.VMEM((tracer_count, columns, levels), f32),
            pltpu.VMEM((levels * groups, LANE), f32),
            pltpu.VMEM((levels * groups, LANE), f32),
            pltpu.VMEM((levels * groups, LANE), f32),
            dma((devices,)),
            dma((devices,)),
            dma((tracer_count,)),
            dma((tracer_count,)),
            dma((3,)),
        ],
        compiler_params=pltpu.CompilerParams(
            collective_id=1, has_side_effects=True, vmem_limit_bytes=limit
        ),
        name="tracers",
    )(flat, mix, inverse, outgoing.reshape(devices, capacity, levels))
    return wave_after, after.reshape(tracers.shape), span[None]


def solution(mesh):
    in_specs = (
        P(None, "gy", "gx", None),
        P(None, "gy", "gx", None),
        P("gy", "gx", None),
        P("gy", "gx"),
        P("gy", "gx"),
    )
    out_specs = (
        P(None, "gy", "gx", None),
        P(None, "gy", "gx", None),
        P(("gx", "gy"), None, None, None),
    )
    return jax.shard_map(
        functools.partial(per_device, mesh.shape["gx"], mesh.shape["gy"]),
        mesh=mesh,
        in_specs=in_specs,
        out_specs=out_specs,
        check_vma=False,
    )
```

```python
import functools

import jax
import jax.numpy as jnp
from jax import lax
from jax.experimental import pallas as pl
from jax.experimental.pallas import tpu as pltpu
from jax.sharding import PartitionSpec as P

SUBSTEPS = 4
COURANT = 0.6
HALO = 4
LANE = 128
MESH = pl.DeviceIdType.MESH
ANY = pl.BlockSpec(memory_space=pl.ANY)
HBM = pl.BlockSpec(memory_space=pltpu.HBM)
VMEM = pl.BlockSpec(memory_space=pltpu.VMEM)
SMEM = pl.BlockSpec(memory_space=pltpu.SMEM)


def exchange_kernel(
    ngx, ngy, wave_ref, tracers_ref, padded_ref, total_ref, loaded, send_sem, recv_sem, load_sem
):
    gx = lax.axis_index("gx")
    gy = lax.axis_index("gy")
    rows, cols = wave_ref.shape[1:3]
    tracer_count = tracers_ref.shape[0]
    groups = total_ref.shape[0] // LANE
    east = lax.rem(gx + 1, ngx)
    west = lax.rem(gx + ngx - 1, ngx)
    own = pltpu.make_async_copy(
        wave_ref,
        padded_ref.at[:, pl.ds(HALO, rows), pl.ds(8, cols), :],
        load_sem.at[tracer_count],
    )
    own.start()
    loads = [
        pltpu.make_async_copy(tracers_ref.at[t], loaded.at[t], load_sem.at[t])
        for t in range(tracer_count)
    ]
    for load in loads:
        load.start()

    barrier = pltpu.get_barrier_semaphore()
    for there in (west, east):
        pl.semaphore_signal(barrier, inc=1, device_id=(there, gy), device_id_type=MESH)

    @pl.when(gy > 0)
    def _():
        for there in (west, gx, east):
            pl.semaphore_signal(barrier, inc=1, device_id=(there, gy - 1), device_id_type=MESH)

    @pl.when(gy < ngy - 1)
    def _():
        for there in (west, gx, east):
            pl.semaphore_signal(barrier, inc=1, device_id=(there, gy + 1), device_id_type=MESH)

    peers = 2 + jnp.where(gy > 0, 3, 0) + jnp.where(gy < ngy - 1, 3, 0)
    pl.semaphore_wait(barrier, peers)
    own.wait()

    lon_parts = {
        -1: (pl.ds(8, 8), pl.ds(cols + 8, 8)),
        0: (pl.ds(8, cols), pl.ds(8, cols)),
        1: (pl.ds(cols, 8), pl.ds(0, 8)),
    }
    lat_parts = {
        -1: (pl.ds(HALO, HALO), pl.ds(rows + HALO, HALO)),
        0: (pl.ds(HALO, rows), pl.ds(HALO, rows)),
        1: (pl.ds(rows, HALO), pl.ds(0, HALO)),
    }
    lon_device = {-1: west, 0: gx, 1: east}

    def copy_to(dy, dx):
        index = (dy + 1) * 3 + dx + 1
        lat_from, lat_to = lat_parts[dy]
        lon_from, lon_to = lon_parts[dx]
        return pltpu.make_async_remote_copy(
            src_ref=padded_ref.at[:, lat_from, lon_from, :],
            dst_ref=padded_ref.at[:, lat_to, lon_to, :],
            send_sem=send_sem.at[index],
            recv_sem=recv_sem.at[index],
            device_id=(lon_device[dx], gy + dy),
            device_id_type=MESH,
        )

    @pl.when(gy > 0)
    def _():
        for dx in (0, -1, 1):
            copy_to(-1, dx).start()

    @pl.when(gy < ngy - 1)
    def _():
        for dx in (0, -1, 1):
            copy_to(1, dx).start()

    for dx in (-1, 1):
        copy_to(0, dx).start()

    for load in loads:
        load.wait()

    def transpose_group(b, carry):
        part = pl.ds(pl.multiple_of(b * LANE, LANE), LANE)
        value = loaded[0, part, :]
        for t in range(1, tracer_count):
            value = value + loaded[t, part, :]
        total_ref[pl.ds(b, LANE, stride=groups), :] = value.T
        return carry

    lax.fori_loop(0, groups, transpose_group, 0)
    for dx in (-1, 1):
        copy_to(0, dx).wait()

    @pl.when(gy > 0)
    def _():
        for dx in (0, -1, 1):
            copy_to(-1, dx).wait_send()
            copy_to(1, dx).wait_recv()

    @pl.when(gy < ngy - 1)
    def _():
        for dx in (0, -1, 1):
            copy_to(1, dx).wait_send()
            copy_to(-1, dx).wait_recv()


def column_kernel(
    ngy,
    padded_ref,
    eddy_ref,
    class_ref,
    slot_ref,
    total_ref,
    wave_ref,
    mix_ref,
    inverse_ref,
    outgoing_ref,
    field,
    change,
    solved,
    sem,
):
    gy = lax.axis_index("gy")
    rows, cols, levels = eddy_ref.shape
    groups = rows * cols // LANE
    per_group = LANE // cols
    wide = cols + 16
    load = pltpu.make_async_copy(padded_ref, field.at[:, :, pl.ds(8, wide), :], sem)
    load.start()
    outgoing_ref[...] = jnp.zeros_like(outgoing_ref)
    load.wait()

    @pl.when(gy == 0)
    def _():
        field[:, pl.ds(0, HALO)] = jnp.zeros((3, HALO, wide + 16, levels), jnp.float32)

    @pl.when(gy == ngy - 1)
    def _():
        field[:, pl.ds(rows + HALO, HALO)] = jnp.zeros((3, HALO, wide + 16, levels), jnp.float32)

    here = pl.ds(8, wide)
    for step in range(SUBSTEPS):
        low = jnp.where(gy == 0, HALO, step + 1)
        high = jnp.where(gy == ngy - 1, rows + HALO, rows + 2 * HALO - 1 - step)
        north_before = field[2, low - 1, here] - COURANT * (
            field[0, low, here] - field[0, low - 1, here]
        )

        def one_row(i, north_below):
            press = field[0, i, here]
            east = field[1, i, here] - COURANT * (field[0, i, pl.ds(9, wide)] - press)
            north = field[2, i, here] - COURANT * (field[0, i + 1, here] - press)
            field[1, i, here] = east
            field[2, i, here] = north
            east_below = field[1, i, pl.ds(7, wide)]
            field[0, i, here] = press - COURANT * ((east - east_below) + (north - north_below))
            return north

        lax.fori_loop(low, high, one_row, north_before)

    lane = lax.broadcasted_iota(jnp.int32, (cols, levels), 1)
    own = pl.ds(16, cols)

    def one_group(b, carry):
        parts = []
        for r in range(per_group):
            i = b * per_group + r
            east = field[1, i + HALO, own]
            north = field[2, i + HALO, own]
            wave_ref[0, i] = field[0, i + HALO, own]
            wave_ref[1, i] = east
            wave_ref[2, i] = north
            shear = jnp.abs(pltpu.roll(east, levels - 1, 1) - east) + jnp.abs(
                pltpu.roll(north, levels - 1, 1) - north
            )
            parts.append(eddy_ref[i] * (1.0 + jnp.where(lane < levels - 1, shear, 0.0)))
        mix_ref[pl.ds(b, levels, stride=groups), :] = jnp.concatenate(parts, 0).T
        return carry

    lax.fori_loop(0, groups, one_group, 0)

    classes = [class_ref[pl.ds(r, groups, stride=per_group), :] for r in range(per_group)]
    scale = 1.0 + jnp.concatenate(classes, 1).astype(jnp.float32)

    def level_rows(k):
        return pl.ds(pl.multiple_of(k * groups, groups), groups)

    def forward(k, carry):
        ratio_s, mix_below, value_below = carry
        at = level_rows(k)
        mix = jnp.where(k < levels - 1, mix_ref[at, :] * scale, 0.0)
        diagonal = 1.0 + ratio_s
        inverse = 1.0 / (diagonal + mix)
        value = (total_ref[at, :] + mix_below * value_below) * inverse
        mix_ref[at, :] = mix
        inverse_ref[at, :] = inverse
        solved[at, :] = value
        return mix * diagonal * inverse, mix, value

    zero = jnp.zeros((groups, LANE), jnp.float32)
    lax.fori_loop(0, levels, forward, (zero, zero, zero), unroll=4)

    def backward(n, above):
        at = level_rows(levels - 1 - n)
        value = solved[at, :] + mix_ref[at, :] * inverse_ref[at, :] * above
        solved[at, :] = value - total_ref[at, :]
        return value

    lax.fori_loop(0, levels, backward, zero, unroll=8)

    def back_group(b, carry):
        part = pl.ds(pl.multiple_of(b * LANE, LANE), LANE)
        change[part, :] = solved[pl.ds(b, levels, stride=groups), :].T
        return carry

    lax.fori_loop(0, groups, back_group, 0)

    def place(i, carry):
        for j in range(cols):
            outgoing_ref[pl.ds(slot_ref[i, j], 1), :] = change[pl.ds(i * cols + j, 1), :]
        return carry

    lax.fori_loop(0, rows, place, 0)


def tracer_kernel(
    ngx,
    ngy,
    tracers_ref,
    mix_hbm,
    inverse_hbm,
    outgoing_ref,
    after_ref,
    span_ref,
    loaded,
    work,
    mix_ref,
    inverse_ref,
    send_sem,
    recv_sem,
    load_sem,
    own_sem,
):
    devices = ngx * ngy
    gx = lax.axis_index("gx")
    gy = lax.axis_index("gy")
    me = gx * ngy + gy
    tracer_count, columns, levels = tracers_ref.shape
    groups = columns // LANE
    loads = [pltpu.make_async_copy(mix_hbm, mix_ref, own_sem.at[0])]
    loads.append(pltpu.make_async_copy(inverse_hbm, inverse_ref, own_sem.at[1]))
    own = pltpu.make_async_copy(outgoing_ref.at[me], span_ref.at[me], own_sem.at[2])

    def tracer_in(t):
        return pltpu.make_async_copy(tracers_ref.at[t], loaded.at[t], load_sem.at[t])

    def partner(n):
        px = lax.rem(gx + n // ngy, ngx)
        py = lax.rem(gy + lax.rem(n, ngy), ngy)
        return px, py

    barrier = pltpu.get_barrier_semaphore()

    def greet(n, carry):
        pl.semaphore_signal(barrier, inc=1, device_id=partner(n), device_id_type=MESH)
        return carry

    lax.fori_loop(1, devices, greet, 0)
    for load in loads:
        load.start()
    own.start()
    for t in range(tracer_count):
        tracer_in(t).start()
    pl.semaphore_wait(barrier, devices - 1)

    def send(n):
        px, py = partner(n)
        return pltpu.make_async_remote_copy(
            src_ref=outgoing_ref.at[px * ngy + py],
            dst_ref=span_ref.at[me],
            send_sem=send_sem.at[n],
            recv_sem=recv_sem.at[n],
            device_id=(px, py),
            device_id_type=MESH,
        )

    def start_send(n, carry):
        send(n).start()
        return carry

    lax.fori_loop(1, devices, start_send, 0)
    for load in loads:
        load.wait()
    zero = jnp.zeros((groups, LANE), jnp.float32)

    def level_rows(k):
        return pl.ds(pl.multiple_of(k * groups, groups), groups)

    def one_tracer(t, carry):
        tracer_in(t).wait()

        def turn(b, carry):
            part = pl.ds(pl.multiple_of(b * LANE, LANE), LANE)
            work[pl.ds(b, levels, stride=groups), :] = loaded[t, part, :].T
            return carry

        lax.fori_loop(0, groups, turn, 0)

        def forward(k, carry):
            mix_below, value_below = carry
            at = level_rows(k)
            value = (work[at, :] + mix_below * value_below) * inverse_ref[at, :]
            work[at, :] = value
            return mix_ref[at, :], value

        lax.fori_loop(0, levels, forward, (zero, zero), unroll=8)

        def backward(n, above):
            at = level_rows(levels - 1 - n)
            value = work[at, :] + mix_ref[at, :] * inverse_ref[at, :] * above
            work[at, :] = value
            return value

        lax.fori_loop(0, levels, backward, zero, unroll=8)

        def turn_back(b, carry):
            part = pl.ds(pl.multiple_of(b * LANE, LANE), LANE)
            after_ref[t, part, :] = work[pl.ds(b, levels, stride=groups), :].T
            return carry

        lax.fori_loop(0, groups, turn_back, 0)
        return carry

    lax.fori_loop(0, tracer_count, one_tracer, 0)

    own.wait()

    def finish(n, carry):
        send(n).wait()
        return carry

    lax.fori_loop(1, devices, finish, 0)


def per_device(ngx, ngy, wave_state, tracers, eddy, cost_class, span_slot):
    rows, cols, levels = eddy.shape
    columns = rows * cols
    groups = columns // LANE
    devices = ngx * ngy
    capacity = max(2, (2 * columns + devices - 1) // devices)
    tracer_count = tracers.shape[0]
    f32 = jnp.float32
    flat = pltpu.with_memory_space_constraint(tracers.reshape(tracer_count, columns, levels), pltpu.HBM)
    wave_state = pltpu.with_memory_space_constraint(wave_state, pltpu.HBM)
    turned = jax.ShapeDtypeStruct((levels * groups, LANE), f32)
    dma = pltpu.SemaphoreType.DMA
    mib = 2**20

    padded, total = pl.pallas_call(
        functools.partial(exchange_kernel, ngx, ngy),
        out_shape=(
            jax.ShapeDtypeStruct((3, rows + 2 * HALO, cols + 16, levels), f32),
            turned,
        ),
        in_specs=[HBM, HBM],
        out_specs=(VMEM, VMEM),
        scratch_shapes=[
            pltpu.VMEM((tracer_count, columns, levels), f32),
            dma((9,)),
            dma((9,)),
            dma((tracer_count + 1,)),
        ],
        compiler_params=pltpu.CompilerParams(
            collective_id=0, has_side_effects=True, vmem_limit_bytes=16 * mib
        ),
        name="exchange",
    )(wave_state, flat)

    wave_after, mix, inverse, outgoing = pl.pallas_call(
        functools.partial(column_kernel, ngy),
        out_shape=(
            jax.ShapeDtypeStruct(wave_state.shape, f32),
            turned,
            turned,
            jax.ShapeDtypeStruct((devices * capacity, levels), f32),
        ),
        in_specs=[ANY, VMEM, VMEM, SMEM, VMEM],
        out_specs=(VMEM, VMEM, VMEM, VMEM),
        scratch_shapes=[
            pltpu.VMEM((3, rows + 2 * HALO, cols + 32, levels), f32),
            pltpu.VMEM((columns, levels), f32),
            pltpu.VMEM((levels * groups, LANE), f32),
            dma(()),
        ],
        compiler_params=pltpu.CompilerParams(vmem_limit_bytes=24 * mib),
        name="columns",
    )(padded, eddy, cost_class, span_slot, total)

    after, span = pl.pallas_call(
        functools.partial(tracer_kernel, ngx, ngy),
        out_shape=(
            jax.ShapeDtypeStruct((tracer_count, columns, levels), f32),
            jax.ShapeDtypeStruct((devices, capacity, levels), f32),
        ),
        in_specs=[HBM, ANY, ANY, ANY],
        out_specs=(VMEM, ANY),
        scratch_shapes=[
            pltpu.VMEM((tracer_count, columns, levels), f32),
            pltpu.VMEM((levels * groups, LANE), f32),
            pltpu.VMEM((levels * groups, LANE), f32),
            pltpu.VMEM((levels * groups, LANE), f32),
            dma((devices,)),
            dma((devices,)),
            dma((tracer_count,)),
            dma((3,)),
        ],
        compiler_params=pltpu.CompilerParams(
            collective_id=1, has_side_effects=True, vmem_limit_bytes=17 * mib
        ),
        name="tracers",
    )(flat, mix, inverse, outgoing.reshape(devices, capacity, levels))
    return wave_after, after.reshape(tracers.shape), span[None]


def solution(mesh):
    in_specs = (
        P(None, "gy", "gx", None),
        P(None, "gy", "gx", None),
        P("gy", "gx", None),
        P("gy", "gx"),
        P("gy", "gx"),
    )
    out_specs = (
        P(None, "gy", "gx", None),
        P(None, "gy", "gx", None),
        P(("gx", "gy"), None, None, None),
    )
    return jax.shard_map(
        functools.partial(per_device, mesh.shape["gx"], mesh.shape["gy"]),
        mesh=mesh,
        in_specs=in_specs,
        out_specs=out_specs,
        check_vma=False,
    )
```
